512 devices in a mesh: cfg: 2 (over core), clip: 8 (over x, z_hi), sp: 32 (over z_lo, y).
Axes of the slice: x: 4, y: 8, z: 8 (z_hi: 2, z_lo: 4; z = z_hi * 4 + z_lo), core: 2. Of those that a mesh axis runs over, the one named last changes fastest.
Arguments:
- self_queries: bfloat16 [8, 2, 2560, 4096], P('clip', 'cfg', 'sp'), may hold values from -256 to 256
- self_keys: bfloat16 [8, 2, 2560, 4096], P('clip', 'cfg', 'sp'), may hold values from -8 to 8
- self_values: bfloat16 [8, 2, 2560, 4096], P('clip', 'cfg', 'sp'), may hold values from -6 to 6
- cross_queries: bfloat16 [8, 2, 2560, 4096], P('clip', 'cfg', 'sp'), may hold values from -256 to 256
- text_keys: bfloat16 [2, 512, 4096], P('cfg', 'clip', 'sp'), may hold values from -8 to 8
- text_values: bfloat16 [2, 512, 4096], P('cfg', 'clip', 'sp'), may hold values from -6 to 6
- text_lengths: int32 [2], P('cfg'), may hold values from 64 to 512, as said below
- head_weight: bfloat16 [4096, 64], replicated, may hold values from -0.09375 to 0.09375
- latent: float32 [8, 2560, 64], P('clip', 'sp', 'cfg'), may hold values from -6 to 6
- previous_denoised: float32 [8, 2560, 64], P('clip', 'sp', 'cfg'), may hold values from -6 to 6
- step_index: int32 [8], P('clip'), may hold values from 2 to 48
Outputs:
- denoised: float32 [8, 2560, 64], P('clip', 'sp', 'cfg')
- next_latent: float32 [8, 2560, 64], P('clip', 'sp', 'cfg')
The draws below stay inside these ranges and needn't reach their ends.
Inputs may be any that keep to these rules, and one draw needn't show every extreme that they name: `text_lengths`: one of the two branches uses all 512 prompt tokens.
All inputs are finite; a program needn't handle non-finite values.
Results may differ from the reference program's by a relative error of at most 0.0009.
The reference program's roundings to bfloat16 on the way count: a program that leaves them out, or rounds other values in their place, can miss the bound.
Values may be sent and summed in bfloat16 or wider, within the bound.
A program may use at most 64 MiB of HBM per device.

```python
import math
import jax
import jax.numpy as jnp
from jax import lax

HEADS = 32
HEAD_SIZE = 128
LAT = 64
TXT = 512
STEPS = 50
HH = 4096
SEQ = 2560
CLIPS = 8


strengths = (120.0, 180.0, 250.0, 320.0, 400.0, 150.0)


def key_table(key, shape, spacing):
    table = jnp.clip(jax.random.normal(key, shape, jnp.float32) * 1.6, -8.0, 8.0)
    for pair_index in range(len(strengths)):
        first = pair_index * spacing
        table = table.at[..., first + 1, :].set(table[..., first + 1, :])
    return table


def self_table(key):
    return key_table(jax.random.fold_in(key, 101), (CLIPS, 2, SEQ, HH), SEQ // 6)


def prompt_table(key):
    return key_table(jax.random.fold_in(key, 202), (2, TXT, HH), TXT // 8 // 6)


def draw_self_keys(key, part):
    return self_table(key).astype(jnp.bfloat16)


def draw_text_keys(key, part):
    return prompt_table(key).astype(jnp.bfloat16)


def draw_self_queries(key, part):
    key = jax.random.fold_in(key, 1)
    queries = jnp.clip(jax.random.normal(key, (CLIPS, 2, SEQ, HH), jnp.float32) * 1.6, -8.0, 8.0)
    return queries.astype(jnp.bfloat16)


def draw_cross_queries(key, part):
    key = jax.random.fold_in(key, 2)
    queries = jnp.clip(jax.random.normal(key, (CLIPS, 2, SEQ, HH), jnp.float32) * 1.6, -8.0, 8.0)
    return queries.astype(jnp.bfloat16)


def draw_text_lengths(key, part):
    key = jax.random.fold_in(key, 5)
    shorter = jax.random.randint(key, (), TXT // 8, TXT + 1)
    flipped = jax.random.randint(jax.random.fold_in(key, 6), (), 0, 2)
    return jnp.where(jnp.arange(2) == flipped, TXT, shorter).astype(jnp.int32)


def set_ends(entries, stream_key, low, top_value):
    index_at = [jax.random.randint(jax.random.fold_in(stream_key, axis), (), 0, length) for axis, length in enumerate(entries.shape)]
    longest = entries.shape.index(max(entries.shape))
    beside = index_at[:longest] + [(index_at[longest] + 1) % entries.shape[longest]] + index_at[longest + 1:]
    return entries.at[tuple(index_at)].set(low).at[tuple(beside)].set(top_value)


def block_scale(key, shape, pieces, low, largest):
    loudness = 1.0
    for axis_at, shards_of in pieces:
        heights = jax.random.uniform(jax.random.fold_in(jax.random.fold_in(key, 6), axis_at), (shards_of,), jnp.float32, low / len(pieces), largest / len(pieces))
        loudness = loudness * jnp.repeat(jnp.exp(heights), shape[axis_at] // shards_of).reshape((-1,) + (1,) * (len(shape) - 1 - axis_at))
    return loudness


def bell_draw(rng, dims, width, limit, cuts=(), kind=jnp.bfloat16):
    result = jax.random.normal(rng, dims, jnp.float32) * width
    if len(cuts) > 0:
        result = block_scale(rng, dims, cuts, -0.22, 0.18) * result
    return jnp.clip(result, min=-limit, max=limit).astype(kind)


def setup_inputs(seed: int = 0) -> dict:
    key_of = jax.random.split(jax.random.key(seed), 12)
    return {
        "self_queries": draw_self_queries(jax.random.fold_in(key_of[11], 71), 0),
        "self_keys": draw_self_keys(jax.random.fold_in(key_of[11], 71), 0),
        "self_values": bell_draw(key_of[2], (CLIPS, 2, SEQ, HH), 1.0, 6.0, ((0, 8), (1, 2), (2, 32))),
        "cross_queries": draw_cross_queries(jax.random.fold_in(key_of[11], 71), 0),
        "text_keys": draw_text_keys(jax.random.fold_in(key_of[11], 71), 0),
        "text_values": bell_draw(key_of[5], (2, TXT, HH), 1.0, 6.0, ((0, 2), (1, 8), (2, 32))),
        "text_lengths": draw_text_lengths(jax.random.fold_in(key_of[11], 71), 0),
        "head_weight": bell_draw(key_of[7], (HH, LAT), HH ** -0.5, 0.09375),
        "latent": bell_draw(key_of[8], (CLIPS, SEQ, LAT), 1.0, 6.0, ((0, 8), (1, 32), (2, 2)), jnp.float32),
        "previous_denoised": bell_draw(key_of[9], (CLIPS, SEQ, LAT), 1.0, 6.0, ((0, 8), (1, 32), (2, 2)), jnp.float32),
        "step_index": set_ends(jax.random.randint(key_of[10], (CLIPS,), 2, STEPS - 1), jax.random.fold_in(key_of[10], 1), 2, (STEPS - 1) - 1).astype(jnp.int32),
    }


guide_scale = 5.0
shift_factor = 5.0

def softmax_rows(scores):
    row_max = lax.optimization_barrier(jnp.max(scores, axis=-1, keepdims=True))
    shifted = jnp.exp(scores - row_max)
    return (shifted / lax.optimization_barrier(jnp.sum(shifted, axis=-1, keepdims=True))).astype(jnp.bfloat16)

def one_head(inputs):
    query_rows, key_rows, value_rows, cross_rows, prompt_keys, prompt_values, text_limit = inputs
    scale = 1.0 / math.sqrt(HEAD_SIZE)
    scores = jnp.dot(query_rows, key_rows.T, preferred_element_type=jnp.float32) * scale
    self_out = jnp.dot(softmax_rows(scores), value_rows, preferred_element_type=jnp.float32)
    cross = jnp.dot(cross_rows, prompt_keys.T, preferred_element_type=jnp.float32) * scale
    cross = jnp.where(jnp.arange(TXT, dtype=jnp.int32)[None, :] < text_limit, cross, -1e+30)
    cross_out = jnp.dot(softmax_rows(cross), prompt_values, preferred_element_type=jnp.float32)
    return (self_out + cross_out).astype(jnp.bfloat16)

def split_heads(matrix):
    return matrix.reshape(matrix.shape[0], HEADS, HEAD_SIZE).transpose(1, 0, 2)

def one_branch(inputs):
    query_rows, key_rows, value_rows, cross_rows, prompt_keys, prompt_values, text_limit = inputs
    limits = jnp.full((HEADS,), text_limit, jnp.int32)
    outputs = lax.map(one_head, (split_heads(query_rows), split_heads(key_rows), split_heads(value_rows), split_heads(cross_rows), split_heads(prompt_keys), split_heads(prompt_values), limits))
    return outputs.transpose(1, 0, 2).reshape(SEQ, HH)

def sigma_at(position):
    level = 1.0 - position / STEPS
    return shift_factor * level / (1.0 + (shift_factor - 1.0) * level)

def log_ratio(sigma_value):
    return jnp.log(1.0 - sigma_value) - jnp.log(sigma_value)

def reference(self_queries, self_keys, self_values, cross_queries, text_keys, text_values, text_lengths, head_weight, latent, previous_denoised, step_index):
    flat = lambda array: array.reshape(CLIPS * 2, SEQ, HH)
    prompt_keys = jnp.broadcast_to(text_keys[None], (CLIPS, 2, TXT, HH)).reshape(CLIPS * 2, TXT, HH)
    prompt_values = jnp.broadcast_to(text_values[None], (CLIPS, 2, TXT, HH)).reshape(CLIPS * 2, TXT, HH)
    limits = jnp.broadcast_to(text_lengths[None], (CLIPS, 2)).reshape(CLIPS * 2).astype(jnp.int32)
    attended = lax.map(one_branch, (flat(self_queries), flat(self_keys), flat(self_values), flat(cross_queries), prompt_keys, prompt_values, limits)).reshape(CLIPS, 2, SEQ, HH)
    conditional = attended[:, 0].astype(jnp.float32)
    unconditional = attended[:, 1].astype(jnp.float32)
    guided = unconditional + guide_scale * (conditional - unconditional)
    weight_full = head_weight.astype(jnp.float32)
    velocity = lax.map(lambda rows: jnp.dot(rows, weight_full, precision=lax.Precision.HIGHEST, preferred_element_type=jnp.float32), guided)
    position = step_index.astype(jnp.float32)
    sigma_now = sigma_at(position)[:, None, None]
    sigma_next = sigma_at(position + 1.0)[:, None, None]
    sigma_prev = sigma_at(position - 1.0)[:, None, None]
    denoised = latent - sigma_now * velocity
    lambda_now = log_ratio(sigma_now)
    h_value = log_ratio(sigma_next) - lambda_now
    phi_value = jnp.expm1(-h_value)
    ratio = (log_ratio(sigma_prev) - lambda_now) / h_value
    difference = (denoised - previous_denoised) / ratio
    next_latent = sigma_next / sigma_now * latent - (1.0 - sigma_next) * phi_value * denoised - 0.5 * (1.0 - sigma_next) * phi_value * difference
    return (denoised, next_latent)
```

```python
import math

import jax
import jax.numpy as jnp
from jax import lax
from jax.experimental import pallas as pl
from jax.experimental.pallas import tpu as pltpu
from jax.sharding import PartitionSpec as P

HEAD_SIZE = 128
STEPS = 50
MESH = pl.DeviceIdType.MESH

guide_scale = 5.0
shift_factor = 5.0

Y = 8
Z = 4
PEERS = Y * Z
TOKENS = 80
PAIRS = PEERS // 2
PACK = 24
SCORE_SCALE = math.log2(math.e) / math.sqrt(HEAD_SIZE)
NT = (((1,), (1,)), ((), ()))
TN = (((0,), (0,)), ((), ()))


def sigma_at(position):
    level = 1.0 - position / STEPS
    return shift_factor * level / (1.0 + (shift_factor - 1.0) * level)


def log_ratio(sigma_value):
    return jnp.log(1.0 - sigma_value) - jnp.log(sigma_value)


def attend(queries, keys, values, text_limit):
    scores = lax.dot_general(queries, keys, NT, preferred_element_type=jnp.float32)
    if text_limit is not None:
        positions = lax.broadcasted_iota(jnp.int32, scores.shape, 1)
        scores = jnp.where(positions < text_limit, scores, -1e30)
    row_max = jnp.max(scores, axis=-1, keepdims=True)
    shifted = jnp.exp2((scores - row_max) * SCORE_SCALE)
    inverse = 1.0 / jnp.sum(shifted, axis=-1, keepdims=True)
    weights = (shifted * inverse).astype(jnp.bfloat16)
    return jnp.dot(weights, values, preferred_element_type=jnp.float32)


def offsets(slot):
    step = lax.rem(PEERS - slot, PEERS)
    ring, dz = lax.div(step, Z), lax.rem(step, Z)
    dy = lax.div(ring + 1, 2) * (2 * lax.rem(ring, 2) - 1)
    return dy, dz


def kernel(
    limit_ref,
    step_ref,
    q_ref,
    k_ref,
    v_ref,
    c_ref,
    tk_ref,
    tv_ref,
    w_ref,
    latent_ref,
    previous_ref,
    denoised_ref,
    next_ref,
    q_buf,
    k_buf,
    v_buf,
    c_buf,
    tk_buf,
    tv_buf,
    w_buf,
    spread,
    mine,
    part_out,
    part_in,
    back_out,
    back_in,
    send_sem,
    recv_sem,
    text_send,
    text_recv,
    local_sem,
    part_send,
    part_recv,
    back_send,
    back_recv,
):
    core = lax.axis_index("cfg")
    clip = lax.axis_index("clip")
    sp = lax.axis_index("sp")
    my_y, my_z = lax.rem(sp, Y), lax.div(sp, Y)
    my_x, my_far = lax.div(clip, 2), lax.rem(clip, 2)
    far_clip = my_x * 2 + (1 - my_far)

    def place(y_at, dz):
        low, high = lax.rem(dz, 2), lax.div(dz, 2)
        z_at = my_z + low * (1 - 2 * lax.rem(my_z, 2)) + 2 * high * (1 - 2 * lax.div(my_z, 2))
        return z_at * Y + lax.rem(y_at + Y, Y)

    def target(slot):
        dy, dz = offsets(slot)
        return place(my_y + dy, dz)

    def origin(slot):
        dy, dz = offsets(slot)
        return place(my_y - dy, dz)

    def x_clip(dx, far):
        return lax.rem(my_x + dx, 4) * 2 + far

    barrier = pltpu.get_barrier_semaphore()

    def greet(slot, carry):
        pl.semaphore_signal(barrier, inc=1, device_id={"sp": target(slot)}, device_id_type=MESH)
        return carry

    lax.fori_loop(1, PEERS, greet, 0)
    pl.semaphore_signal(barrier, inc=1, device_id={"cfg": 1 - core}, device_id_type=MESH)
    pl.semaphore_signal(barrier, inc=1, device_id={"clip": far_clip}, device_id_type=MESH)
    for dx in range(1, 4):
        pl.semaphore_signal(
            barrier, inc=1, device_id={"clip": x_clip(dx, my_far)}, device_id_type=MESH
        )

    def slab(ref, at):
        return ref.at[:, pl.ds(pl.multiple_of(at * HEAD_SIZE, HEAD_SIZE), HEAD_SIZE)]

    pairs = ((k_ref, k_buf), (v_ref, v_buf), (c_ref, c_buf), (q_ref, q_buf))
    for at, (ref, buf) in enumerate(pairs):
        pltpu.make_async_copy(slab(ref, sp), buf.at[0], recv_sem.at[at, 0]).start()
    own_text = [
        pltpu.make_async_copy(tk_ref, tk_buf.at[clip], local_sem.at[0]),
        pltpu.make_async_copy(tv_ref, tv_buf.at[clip], local_sem.at[1]),
    ]
    own_weight = pltpu.make_async_copy(slab(w_ref, sp), w_buf, local_sem.at[2])
    for copy in own_text:
        copy.start()
    own_weight.start()

    pl.semaphore_wait(barrier, PEERS - 1 + 1 + 1 + 3)

    def moved(at, slot):
        ref, buf = pairs[at]
        to = target(slot)
        return pltpu.make_async_remote_copy(
            src_ref=slab(ref, to),
            dst_ref=buf.at[slot],
            send_sem=send_sem.at[at, slot],
            recv_sem=recv_sem.at[at, slot],
            device_id={"sp": to},
            device_id_type=MESH,
        )

    texts = ((tk_ref, tk_buf), (tv_ref, tv_buf))

    def text_copy(at, lane):
        ref, buf = texts[at]
        if lane == 0:
            to, source, chunk = far_clip, ref, clip
        elif lane < 4:
            to, source, chunk = x_clip(lane, my_far), ref, clip
        else:
            to, source, chunk = x_clip(lane - 3, my_far), buf.at[far_clip], far_clip
        return pltpu.make_async_remote_copy(
            src_ref=source,
            dst_ref=buf.at[chunk],
            send_sem=text_send.at[at, lane],
            recv_sem=text_recv.at[at, lane],
            device_id={"clip": to},
            device_id_type=MESH,
        )

    for lane in range(4):
        for at in range(2):
            text_copy(at, lane).start()

    def send_one(at):
        def body(slot, carry):
            moved(at, slot).start()
            return carry

        lax.fori_loop(1, PEERS, body, 0)

    send_one(0)
    for at in range(2):
        text_copy(at, 0).wait_recv()
    for lane in range(4, 7):
        for at in range(2):
            text_copy(at, lane).start()
    send_one(1)

    def send_queries(slot, carry):
        moved(2, slot).start()
        moved(3, slot).start()
        return carry

    lax.fori_loop(1, PEERS, send_queries, 0)

    own_weight.wait()
    weight = w_buf[...]
    for half in range(2):
        for group in range(4):
            channel = lax.broadcasted_iota(jnp.int32, (64, 128), 0) - 32 * half
            lane = lax.broadcasted_iota(jnp.int32, (64, 128), 1) - 32 * group
            chosen = (channel == lane) & (lane >= 0) & (lane < 32)
            chosen = jnp.where(chosen, 1.0, 0.0).astype(jnp.bfloat16)
            spread[pl.ds(group * 128, 128), pl.ds(half * 128, 128)] = lax.dot_general(
                weight, chosen, TN, preferred_element_type=jnp.float32
            ).astype(jnp.bfloat16)

    position = jnp.full((1, TOKENS), step_ref[0], jnp.int32).astype(jnp.float32)
    sigma_now = sigma_at(position)
    sigma_next = sigma_at(position + 1.0)
    sigma_prev = sigma_at(position - 1.0)
    lambda_now = log_ratio(sigma_now)
    h_value = log_ratio(sigma_next) - lambda_now
    phi_value = jnp.exp(-h_value) - 1.0
    ratio = (log_ratio(sigma_prev) - lambda_now) / h_value
    text_limit = limit_ref[0]
    coefficient = jnp.where(core == 0, guide_scale, 1.0 - guide_scale)

    for copy in own_text:
        copy.wait()
    for lane in range(1, 7):
        for at in range(2):
            text_copy(at, lane).wait_recv()

    for at in range(2):
        ref, buf = pairs[at]
        pltpu.make_async_copy(slab(ref, sp), buf.at[0], recv_sem.at[at, 0]).wait()

    def arrived(slot, carry):
        moved(0, slot).wait_recv()
        moved(1, slot).wait_recv()
        return carry

    lax.fori_loop(1, PEERS, arrived, 0)

    def to_partner(pair):
        return pltpu.make_async_remote_copy(
            src_ref=part_out.at[pair],
            dst_ref=part_in.at[pair],
            send_sem=part_send.at[pair],
            recv_sem=part_recv.at[pair],
            device_id={"cfg": 1 - core},
            device_id_type=MESH,
        )

    def to_owner(slot):
        return pltpu.make_async_remote_copy(
            src_ref=back_out.at[slot],
            dst_ref=back_in.at[slot],
            send_sem=back_send.at[slot],
            recv_sem=back_recv.at[slot],
            device_id={"sp": origin(slot)},
            device_id_type=MESH,
        )

    def wait_queries(slot):
        for at in (2, 3):
            moved(at, slot).wait_recv()

    def finish(pair):
        to_partner(pair).wait_recv()
        both = mine[pair] + part_in[pair]
        back_out[2 * pair] = both[:PACK]
        back_out[2 * pair + 1] = both[PACK:]

        @pl.when(pair > 0)
        def _():
            to_owner(2 * pair).start()

        to_owner(2 * pair + 1).start()

    def one_pair(pair, carry):
        @pl.when(pair == 0)
        def _():
            for at in (2, 3):
                ref, buf = pairs[at]
                pltpu.make_async_copy(slab(ref, sp), buf.at[0], recv_sem.at[at, 0]).wait()

        @pl.when(pair > 0)
        def _():
            wait_queries(2 * pair)

        wait_queries(2 * pair + 1)
        rows = 2 * TOKENS
        keys = k_buf[...].reshape(PEERS * TOKENS, HEAD_SIZE)
        values = v_buf[...].reshape(PEERS * TOKENS, HEAD_SIZE)
        queries = q_buf[pl.ds(2 * pair, 2)].reshape(rows, HEAD_SIZE)
        crossing = c_buf[pl.ds(2 * pair, 2)].reshape(rows, HEAD_SIZE)
        prompt_keys = tk_buf[...].reshape(512, HEAD_SIZE)
        prompt_values = tv_buf[...].reshape(512, HEAD_SIZE)
        self_out = attend(queries, keys, values, None)
        cross_out = attend(crossing, prompt_keys, prompt_values, text_limit)
        attended = (self_out + cross_out).astype(jnp.bfloat16).astype(jnp.float32)
        packed = []
        for first in (0, TOKENS):
            groups = [attended[first + PACK * g : first + PACK * (g + 1)] for g in range(3)]
            last = attended[first + 3 * PACK : first + TOKENS]
            padding = jnp.zeros((4 * PACK - TOKENS, HEAD_SIZE), jnp.float32)
            groups.append(jnp.concatenate([last, padding], axis=0))
            packed.append(jnp.concatenate(groups, axis=1))
        packed = jnp.concatenate(packed, axis=0).astype(jnp.bfloat16)
        product = coefficient * jnp.dot(packed, spread[...], preferred_element_type=jnp.float32)
        low, high = product[:, :128], product[:, 128:]
        mine[pair] = jnp.where(core == 0, low, high)
        part_out[pair] = jnp.where(core == 0, high, low)
        to_partner(pair).start()

        @pl.when(pair > 0)
        def _():
            finish(pair - 1)

        return carry

    lax.fori_loop(0, PAIRS, one_pair, 0)
    finish(PAIRS - 1)

    def returned(slot, carry):
        to_owner(slot).wait_recv()
        return carry + back_in[slot]

    total = lax.fori_loop(1, PEERS, returned, back_out[0])
    square = jnp.concatenate([total, jnp.zeros((128 - PACK, 128), jnp.float32)], axis=0).T
    token = lax.broadcasted_iota(jnp.int32, (32, 128), 1)
    velocity = square[:32]
    for group in range(1, 4):
        shifted = pltpu.roll(square[32 * group : 32 * (group + 1)], PACK * group, 1)
        velocity = jnp.where(token < PACK * group, velocity, shifted)
    velocity = velocity[:, :TOKENS]
    latent = latent_ref[...]
    denoised = latent - sigma_now * velocity
    difference = (denoised - previous_ref[...]) / ratio
    denoised_ref[...] = denoised
    next_ref[...] = (
        sigma_next / sigma_now * latent
        - (1.0 - sigma_next) * phi_value * denoised
        - 0.5 * (1.0 - sigma_next) * phi_value * difference
    )

    def sent(slot, carry):
        for at in range(4):
            moved(at, slot).wait_send()
        to_owner(slot).wait_send()
        return carry

    lax.fori_loop(1, PEERS, sent, 0)
    for lane in range(7):
        for at in range(2):
            text_copy(at, lane).wait_send()

    def part_sent(pair, carry):
        to_partner(pair).wait_send()
        return carry

    lax.fori_loop(0, PAIRS, part_sent, 0)


def on_device(
    self_queries,
    self_keys,
    self_values,
    cross_queries,
    text_keys,
    text_values,
    text_lengths,
    head_weight,
    latent,
    previous_denoised,
    step_index,
):
    flat = lambda array: array.reshape(array.shape[-2], array.shape[-1])
    vmem = pl.BlockSpec(memory_space=pltpu.VMEM)
    smem = pl.BlockSpec(memory_space=pltpu.SMEM)
    anywhere = pl.BlockSpec(memory_space=pl.ANY)
    block = pltpu.VMEM((PEERS, TOKENS, HEAD_SIZE), jnp.bfloat16)
    prompt = pltpu.VMEM((8, 64, HEAD_SIZE), jnp.bfloat16)
    paired = pltpu.VMEM((PAIRS, 2 * PACK, 128), jnp.float32)
    single = pltpu.VMEM((PEERS, PACK, 128), jnp.float32)
    dma = pltpu.SemaphoreType.DMA
    out = jax.ShapeDtypeStruct((32, TOKENS), jnp.float32)
    denoised, next_latent = pl.pallas_call(
        kernel,
        out_shape=(out, out),
        in_specs=[smem, smem] + [anywhere] * 7 + [vmem] * 2,
        out_specs=(vmem, vmem),
        scratch_shapes=[block] * 4
        + [prompt] * 2
        + [pltpu.VMEM((64, HEAD_SIZE), jnp.bfloat16), pltpu.VMEM((512, 256), jnp.bfloat16)]
        + [paired] * 3
        + [single] * 2
        + [dma((4, PEERS)), dma((4, PEERS)), dma((2, 7)), dma((2, 7)), dma((3,))]
        + [dma((PAIRS,)), dma((PAIRS,)), dma((PEERS,)), dma((PEERS,))],
        compiler_params=pltpu.CompilerParams(
            collective_id=0, has_side_effects=True, vmem_limit_bytes=62 * 2**20
        ),
        name="denoise",
    )(
        text_lengths,
        step_index,
        flat(self_queries),
        flat(self_keys),
        flat(self_values),
        flat(cross_queries),
        flat(text_keys),
        flat(text_values),
        head_weight.T,
        flat(latent).T,
        flat(previous_denoised).T,
    )
    return (denoised.T[None], next_latent.T[None])


def solution(mesh):
    return jax.shard_map(
        on_device,
        mesh=mesh,
        in_specs=(
            P("clip", "cfg", "sp", None),
            P("clip", "cfg", "sp", None),
            P("clip", "cfg", "sp", None),
            P("clip", "cfg", "sp", None),
            P("cfg", "clip", "sp"),
            P("cfg", "clip", "sp"),
            P("cfg"),
            P(),
            P("clip", "sp", "cfg"),
            P("clip", "sp", "cfg"),
            P("clip"),
        ),
        out_specs=(P("clip", "sp", "cfg"), P("clip", "sp", "cfg")),
        check_vma=False,
    )
```

```python
import math

import jax
import jax.numpy as jnp
from jax import lax
from jax.experimental import pallas as pl
from jax.experimental.pallas import tpu as pltpu
from jax.sharding import PartitionSpec as P

HEAD_SIZE = 128
STEPS = 50
MESH = pl.DeviceIdType.MESH

guide_scale = 5.0
shift_factor = 5.0

Y = 8
Z = 4
PEERS = Y * Z
TOKENS = 80
PAIRS = PEERS // 2
PACK = 24
SCORE_SCALE = math.log2(math.e) / math.sqrt(HEAD_SIZE)
NT = (((1,), (1,)), ((), ()))
TN = (((0,), (0,)), ((), ()))


def sigma_at(position):
    level = 1.0 - position / STEPS
    return shift_factor * level / (1.0 + (shift_factor - 1.0) * level)


def log_ratio(sigma_value):
    return jnp.log(1.0 - sigma_value) - jnp.log(sigma_value)


def attend(queries, keys, values, text_limit):
    scores = lax.dot_general(queries, keys, NT, preferred_element_type=jnp.float32)
    if text_limit is not None:
        positions = lax.broadcasted_iota(jnp.int32, scores.shape, 1)
        scores = jnp.where(positions < text_limit, scores, -1e30)
    row_max = jnp.max(scores, axis=-1, keepdims=True)
    shifted = jnp.exp2((scores - row_max) * SCORE_SCALE)
    inverse = 1.0 / jnp.sum(shifted, axis=-1, keepdims=True)
    weights = (shifted * inverse).astype(jnp.bfloat16)
    return jnp.dot(weights, values, preferred_element_type=jnp.float32)


def offsets(slot):
    step = lax.rem(PEERS - slot, PEERS)
    ring, dz = lax.div(step, Z), lax.rem(step, Z)
    dy = lax.div(ring + 1, 2) * (2 * lax.rem(ring, 2) - 1)
    return dy, dz


def kernel(
    limit_ref,
    step_ref,
    q_ref,
    k_ref,
    v_ref,
    c_ref,
    tk_ref,
    tv_ref,
    w_ref,
    out_ref,
    q_buf,
    k_buf,
    v_buf,
    c_buf,
    tk_buf,
    tv_buf,
    w_buf,
    spread,
    mine,
    part_out,
    part_in,
    back_out,
    back_in,
    send_sem,
    whole_recv,
    pair_recv,
    text_send,
    text_recv,
    local_sem,
    part_send,
    part_recv,
    back_send,
    back_recv,
):
    core = lax.axis_index("cfg")
    clip = lax.axis_index("clip")
    sp = lax.axis_index("sp")
    my_y, my_z = lax.rem(sp, Y), lax.div(sp, Y)
    my_x, my_far = lax.div(clip, 2), lax.rem(clip, 2)
    far_clip = my_x * 2 + (1 - my_far)

    def place(y_at, dz):
        low, high = lax.rem(dz, 2), lax.div(dz, 2)
        z_at = my_z + low * (1 - 2 * lax.rem(my_z, 2)) + 2 * high * (1 - 2 * lax.div(my_z, 2))
        return z_at * Y + lax.rem(y_at + Y, Y)

    def target(slot):
        dy, dz = offsets(slot)
        return place(my_y + dy, dz)

    def origin(slot):
        dy, dz = offsets(slot)
        return place(my_y - dy, dz)

    def x_clip(dx, far):
        return lax.rem(my_x + dx, 4) * 2 + far

    barrier = pltpu.get_barrier_semaphore()

    def greet(slot, carry):
        pl.semaphore_signal(barrier, inc=1, device_id={"sp": target(slot)}, device_id_type=MESH)
        return carry

    lax.fori_loop(1, PEERS, greet, 0)
    pl.semaphore_signal(barrier, inc=1, device_id={"cfg": 1 - core}, device_id_type=MESH)

    @pl.when(my_far == 0)
    def _():
        pl.semaphore_signal(barrier, inc=1, device_id={"clip": far_clip}, device_id_type=MESH)

    for dx in range(1, 4):
        pl.semaphore_signal(
            barrier, inc=1, device_id={"clip": x_clip(dx, my_far)}, device_id_type=MESH
        )

    def slab(ref, at):
        return ref.at[:, pl.ds(pl.multiple_of(at * HEAD_SIZE, HEAD_SIZE), HEAD_SIZE)]

    def arrival(at, slot):
        return whole_recv.at[at] if at < 2 else pair_recv.at[at - 2, lax.div(slot, 2)]

    def await_bytes(part, sem):
        pltpu.make_async_copy(part, part, sem).wait()

    pairs = ((k_ref, k_buf), (v_ref, v_buf), (c_ref, c_buf), (q_ref, q_buf))
    for at, (ref, buf) in enumerate(pairs):
        pltpu.make_async_copy(slab(ref, sp), buf.at[0], arrival(at, 0)).start()
    pltpu.make_async_copy(tk_ref, tk_buf.at[clip], text_recv.at[0, 1]).start()
    pltpu.make_async_copy(tv_ref, tv_buf.at[clip], text_recv.at[1, 1]).start()
    own_weight = pltpu.make_async_copy(slab(w_ref, sp), w_buf, local_sem.at[0])
    own_weight.start()

    pl.semaphore_wait(barrier, PEERS - 1 + 1 + 3 + my_far)

    def moved(at, slot):
        ref, buf = pairs[at]
        to = target(slot)
        return pltpu.make_async_remote_copy(
            src_ref=slab(ref, to),
            dst_ref=buf.at[slot],
            send_sem=send_sem.at[at],
            recv_sem=arrival(at, slot),
            device_id={"sp": to},
            device_id_type=MESH,
        )

    texts = ((tk_ref, tk_buf), (tv_ref, tv_buf))

    def text_copy(at, lane):
        ref, buf = texts[at]
        if lane == 0:
            to, source, chunk = far_clip, ref, clip
        elif lane < 4:
            to, source, chunk = x_clip(lane, my_far), ref, clip
        else:
            to, source, chunk = x_clip(lane - 3, my_far), buf.at[far_clip], far_clip
        return pltpu.make_async_remote_copy(
            src_ref=source,
            dst_ref=buf.at[chunk],
            send_sem=text_send.at[at],
            recv_sem=text_recv.at[at, min(lane, 1)],
            device_id={"clip": to},
            device_id_type=MESH,
        )

    @pl.when(my_far == 1)
    def _():
        for at in range(2):
            text_copy(at, 0).start()

    for lane in range(1, 4):
        for at in range(2):
            text_copy(at, lane).start()

    def send_one(at):
        def body(slot, carry):
            moved(at, slot).start()
            return carry

        lax.fori_loop(1, PEERS, body, 0)

    send_one(0)
    for at in range(2):
        text_copy(at, 0).wait_recv()

    @pl.when(my_far == 0)
    def _():
        for at in range(2):
            text_copy(at, 0).start()

    for lane in range(4, 7):
        for at in range(2):
            text_copy(at, lane).start()
    send_one(1)

    def send_queries(slot, carry):
        moved(2, slot).start()
        moved(3, slot).start()
        return carry

    lax.fori_loop(1, PEERS, send_queries, 0)

    own_weight.wait()
    weight = w_buf[...]
    for half in range(2):
        for group in range(4):
            channel = lax.broadcasted_iota(jnp.int32, (64, 128), 0) - 32 * half
            lane = lax.broadcasted_iota(jnp.int32, (64, 128), 1) - 32 * group
            chosen = (channel == lane) & (lane >= 0) & (lane < 32)
            chosen = jnp.where(chosen, 1.0, 0.0).astype(jnp.bfloat16)
            spread[pl.ds(group * 128, 128), pl.ds(half * 128, 128)] = lax.dot_general(
                weight, chosen, TN, preferred_element_type=jnp.float32
            ).astype(jnp.bfloat16)

    position = jnp.broadcast_to(step_ref[...], (1, TOKENS)).astype(jnp.float32)
    sigma_now = sigma_at(position)
    sigma_next = sigma_at(position + 1.0)
    lambda_now = log_ratio(sigma_now)
    h_value = log_ratio(sigma_next) - lambda_now
    ratio = (log_ratio(sigma_at(position - 1.0)) - lambda_now) / h_value
    pull = (1.0 - sigma_next) * (jnp.exp(-h_value) - 1.0)
    for at, value in enumerate((sigma_now, sigma_next / sigma_now, pull, 0.5 * pull / ratio)):
        out_ref[32 + at : 33 + at] = value
    out_ref[36:] = jnp.zeros((4, TOKENS), jnp.float32)
    text_limit = limit_ref[...]
    coefficient = jnp.where(core == 0, guide_scale, 1.0 - guide_scale)

    for at, buf in enumerate((tk_buf, tv_buf)):
        await_bytes(buf.at[pl.ds(0, 7)], text_recv.at[at, 1])
    for at, buf in enumerate((k_buf, v_buf)):
        await_bytes(buf, whole_recv.at[at])

    def to_partner(pair):
        return pltpu.make_async_remote_copy(
            src_ref=part_out.at[pair],
            dst_ref=part_in.at[pair],
            send_sem=part_send.at[0],
            recv_sem=part_recv.at[pair],
            device_id={"cfg": 1 - core},
            device_id_type=MESH,
        )

    def to_owner(slot):
        return pltpu.make_async_remote_copy(
            src_ref=back_out.at[slot],
            dst_ref=back_in.at[slot],
            send_sem=back_send.at[0],
            recv_sem=back_recv.at[0],
            device_id={"sp": origin(slot)},
            device_id_type=MESH,
        )

    def finish(pair):
        to_partner(pair).wait_recv()
        both = mine[pair] + part_in[pair]
        back_out[2 * pair] = both[:PACK]
        back_out[2 * pair + 1] = both[PACK:]

        @pl.when(pair > 0)
        def _():
            to_owner(2 * pair).start()

        to_owner(2 * pair + 1).start()

    def one_pair(pair, carry):
        for at, buf in enumerate((c_buf, q_buf)):
            await_bytes(buf.at[pl.ds(2 * pair, 2)], pair_recv.at[at, pair])
        rows = 2 * TOKENS
        keys = k_buf[...].reshape(PEERS * TOKENS, HEAD_SIZE)
        values = v_buf[...].reshape(PEERS * TOKENS, HEAD_SIZE)
        queries = q_buf[pl.ds(2 * pair, 2)].reshape(rows, HEAD_SIZE)
        crossing = c_buf[pl.ds(2 * pair, 2)].reshape(rows, HEAD_SIZE)
        prompt_keys = tk_buf[...].reshape(512, HEAD_SIZE)
        prompt_values = tv_buf[...].reshape(512, HEAD_SIZE)
        self_out = attend(queries, keys, values, None)
        cross_out = attend(crossing, prompt_keys, prompt_values, text_limit)
        attended = (self_out + cross_out).astype(jnp.bfloat16).astype(jnp.float32)
        packed = []
        for first in (0, TOKENS):
            groups = [attended[first + PACK * g : first + PACK * (g + 1)] for g in range(3)]
            last = attended[first + 3 * PACK : first + TOKENS]
            padding = jnp.zeros((4 * PACK - TOKENS, HEAD_SIZE), jnp.float32)
            groups.append(jnp.concatenate([last, padding], axis=0))
            packed.append(jnp.concatenate(groups, axis=1))
        packed = jnp.concatenate(packed, axis=0).astype(jnp.bfloat16)
        product = coefficient * jnp.dot(packed, spread[...], preferred_element_type=jnp.float32)
        low, high = product[:, :128], product[:, 128:]
        mine[pair] = jnp.where(core == 0, low, high)
        part_out[pair] = jnp.where(core == 0, high, low)
        to_partner(pair).start()

        @pl.when(pair > 0)
        def _():
            finish(pair - 1)

        return carry

    lax.fori_loop(0, PAIRS, one_pair, 0)
    finish(PAIRS - 1)

    await_bytes(back_in.at[pl.ds(1, PEERS - 1)], back_recv.at[0])
    total = back_out[0] + jnp.sum(back_in[pl.ds(1, PEERS - 1)], axis=0)
    square = jnp.concatenate([total, jnp.zeros((128 - PACK, 128), jnp.float32)], axis=0).T
    token = lax.broadcasted_iota(jnp.int32, (32, 128), 1)
    velocity = square[:32]
    for group in range(1, 4):
        shifted = pltpu.roll(square[32 * group : 32 * (group + 1)], PACK * group, 1)
        velocity = jnp.where(token < PACK * group, velocity, shifted)
    out_ref[:32] = velocity[:, :TOKENS]

    for at, (ref, buf) in enumerate(pairs):
        await_bytes(buf.at[pl.ds(1, PEERS - 1)], send_sem.at[at])
    for at, buf in enumerate((tk_buf, tv_buf)):
        await_bytes(buf.at[pl.ds(0, 7)], text_send.at[at])
    await_bytes(back_out.at[pl.ds(1, PEERS - 1)], back_send.at[0])
    await_bytes(part_out, part_send.at[0])


def on_device(
    self_queries,
    self_keys,
    self_values,
    cross_queries,
    text_keys,
    text_values,
    text_lengths,
    head_weight,
    latent,
    previous_denoised,
    step_index,
):
    flat = lambda array: array.reshape(array.shape[-2], array.shape[-1])
    vmem = pl.BlockSpec(memory_space=pltpu.VMEM)
    anywhere = pl.BlockSpec(memory_space=pl.ANY)
    block = pltpu.VMEM((PEERS, TOKENS, HEAD_SIZE), jnp.bfloat16)
    prompt = pltpu.VMEM((8, 64, HEAD_SIZE), jnp.bfloat16)
    paired = pltpu.VMEM((PAIRS, 2 * PACK, 128), jnp.float32)
    single = pltpu.VMEM((PEERS, PACK, 128), jnp.float32)
    dma = pltpu.SemaphoreType.DMA
    result = pl.pallas_call(
        kernel,
        out_shape=jax.ShapeDtypeStruct((40, TOKENS), jnp.float32),
        in_specs=[vmem] * 2 + [anywhere] * 7,
        out_specs=vmem,
        scratch_shapes=[block] * 4
        + [prompt] * 2
        + [pltpu.VMEM((64, HEAD_SIZE), jnp.bfloat16), pltpu.VMEM((512, 256), jnp.bfloat16)]
        + [paired] * 3
        + [single] * 2
        + [dma((4,)), dma((2,)), dma((2, PAIRS)), dma((2,)), dma((2, 2)), dma((1,))]
        + [dma((1,)), dma((PAIRS,)), dma((1,)), dma((1,))],
        compiler_params=pltpu.CompilerParams(
            collective_id=0, has_side_effects=True, vmem_limit_bytes=62 * 2**20
        ),
        name="denoise",
    )(
        text_lengths.reshape(1, 1),
        step_index.reshape(1, 1),
        flat(self_queries),
        flat(self_keys),
        flat(self_values),
        flat(cross_queries),
        flat(text_keys),
        flat(text_values),
        head_weight.T,
    )
    velocity = result[:32].T[None]
    sigma_now, keep, pull, push = (result[32 + at][None, :, None] for at in range(4))
    denoised = latent - sigma_now * velocity
    next_latent = keep * latent - pull * denoised - push * (denoised - previous_denoised)
    return (denoised, next_latent)


def solution(mesh):
    return jax.shard_map(
        on_device,
        mesh=mesh,
        in_specs=(
            P("clip", "cfg", "sp", None),
            P("clip", "cfg", "sp", None),
            P("clip", "cfg", "sp", None),
            P("clip", "cfg", "sp", None),
            P("cfg", "clip", "sp"),
            P("cfg", "clip", "sp"),
            P("cfg"),
            P(),
            P("clip", "sp", "cfg"),
            P("clip", "sp", "cfg"),
            P("clip"),
        ),
        out_specs=(P("clip", "sp", "cfg"), P("clip", "sp", "cfg")),
        check_vma=False,
    )
```

```python
import math

import jax
import jax.numpy as jnp
from jax import lax
from jax.experimental import pallas as pl
from jax.experimental.pallas import tpu as pltpu
from jax.sharding import PartitionSpec as P

HEAD_SIZE = 128
STEPS = 50
MESH = pl.DeviceIdType.MESH

guide_scale = 5.0
shift_factor = 5.0

Y = 8
Z = 4
PEERS = Y * Z
TOKENS = 80
PAIRS = PEERS // 2
PACK = 24
SCORE_SCALE = math.log2(math.e) / math.sqrt(HEAD_SIZE)
NT = (((1,), (1,)), ((), ()))
TN = (((0,), (0,)), ((), ()))


def sigma_at(position):
    level = 1.0 - position / STEPS
    return shift_factor * level / (1.0 + (shift_factor - 1.0) * level)


def log_ratio(sigma_value):
    return jnp.log(1.0 - sigma_value) - jnp.log(sigma_value)


def attend(queries, keys, values, text_limit):
    scores = lax.dot_general(queries, keys, NT, preferred_element_type=jnp.float32)
    if text_limit is not None:
        positions = lax.broadcasted_iota(jnp.int32, scores.shape, 1)
        scores = jnp.where(positions < text_limit, scores, -1e30)
    row_max = jnp.max(scores, axis=-1, keepdims=True)
    shifted = jnp.exp2((scores - row_max) * SCORE_SCALE)
    inverse = 1.0 / jnp.sum(shifted, axis=-1, keepdims=True)
    weights = (shifted * inverse).astype(jnp.bfloat16)
    return jnp.dot(weights, values, preferred_element_type=jnp.float32)


def offsets(slot):
    step = lax.rem(PEERS - slot, PEERS)
    ring, dz = lax.div(step, Z), lax.rem(step, Z)
    dy = lax.div(ring + 1, 2) * (2 * lax.rem(ring, 2) - 1)
    return dy, dz


def kernel(
    limit_ref,
    step_ref,
    q_ref,
    k_ref,
    v_ref,
    c_ref,
    tk_ref,
    tv_ref,
    w_ref,
    latent_ref,
    previous_ref,
    out_ref,
    q_buf,
    k_buf,
    v_buf,
    c_buf,
    tk_buf,
    tv_buf,
    w_buf,
    latent_buf,
    previous_buf,
    spread,
    mine,
    part_out,
    part_in,
    back_out,
    back_in,
    send_sem,
    whole_recv,
    pair_recv,
    text_send,
    text_recv,
    local_sem,
    part_send,
    part_recv,
    back_send,
    back_recv,
):
    core = lax.axis_index("cfg")
    clip = lax.axis_index("clip")
    sp = lax.axis_index("sp")
    my_y, my_z = lax.rem(sp, Y), lax.div(sp, Y)
    my_x, my_far = lax.div(clip, 2), lax.rem(clip, 2)
    far_clip = my_x * 2 + (1 - my_far)

    def place(y_at, dz):
        low, high = lax.rem(dz, 2), lax.div(dz, 2)
        z_at = my_z + low * (1 - 2 * lax.rem(my_z, 2)) + 2 * high * (1 - 2 * lax.div(my_z, 2))
        return z_at * Y + lax.rem(y_at + Y, Y)

    def target(slot):
        dy, dz = offsets(slot)
        return place(my_y + dy, dz)

    def origin(slot):
        dy, dz = offsets(slot)
        return place(my_y - dy, dz)

    def x_clip(dx, far):
        return lax.rem(my_x + dx, 4) * 2 + far

    barrier = pltpu.get_barrier_semaphore()

    def greet(slot, carry):
        pl.semaphore_signal(barrier, inc=1, device_id={"sp": target(slot)}, device_id_type=MESH)
        return carry

    lax.fori_loop(1, PEERS, greet, 0)
    pl.semaphore_signal(barrier, inc=1, device_id={"cfg": 1 - core}, device_id_type=MESH)

    @pl.when(my_far == 0)
    def _():
        pl.semaphore_signal(barrier, inc=1, device_id={"clip": far_clip}, device_id_type=MESH)

    for dx in range(1, 4):
        pl.semaphore_signal(
            barrier, inc=1, device_id={"clip": x_clip(dx, my_far)}, device_id_type=MESH
        )

    def slab(ref, at):
        return ref.at[:, pl.ds(pl.multiple_of(at * HEAD_SIZE, HEAD_SIZE), HEAD_SIZE)]

    def arrival(at, slot):
        return whole_recv.at[at] if at < 2 else pair_recv.at[at - 2, lax.div(slot, 2)]

    def await_bytes(part, sem):
        pltpu.make_async_copy(part, part, sem).wait()

    pairs = ((k_ref, k_buf), (v_ref, v_buf), (c_ref, c_buf), (q_ref, q_buf))
    for at, (ref, buf) in enumerate(pairs):
        pltpu.make_async_copy(slab(ref, sp), buf.at[0], arrival(at, 0)).start()
    pltpu.make_async_copy(tk_ref, tk_buf.at[clip], text_recv.at[0, 1]).start()
    pltpu.make_async_copy(tv_ref, tv_buf.at[clip], text_recv.at[1, 1]).start()
    own_weight = pltpu.make_async_copy(slab(w_ref, sp), w_buf, local_sem.at[0])
    own_latent = pltpu.make_async_copy(latent_ref, latent_buf, local_sem.at[1])
    own_previous = pltpu.make_async_copy(previous_ref, previous_buf, local_sem.at[2])
    for copy in (own_weight, own_latent, own_previous):
        copy.start()

    pl.semaphore_wait(barrier, PEERS - 1 + 1 + 3 + my_far)

    def moved(at, slot):
        ref, buf = pairs[at]
        to = target(slot)
        return pltpu.make_async_remote_copy(
            src_ref=slab(ref, to),
            dst_ref=buf.at[slot],
            send_sem=send_sem.at[at],
            recv_sem=arrival(at, slot),
            device_id={"sp": to},
            device_id_type=MESH,
        )

    texts = ((tk_ref, tk_buf), (tv_ref, tv_buf))

    def text_copy(at, lane):
        ref, buf = texts[at]
        if lane == 0:
            to, source, chunk = far_clip, ref, clip
        elif lane < 4:
            to, source, chunk = x_clip(lane, my_far), ref, clip
        else:
            to, source, chunk = x_clip(lane - 3, my_far), buf.at[far_clip], far_clip
        return pltpu.make_async_remote_copy(
            src_ref=source,
            dst_ref=buf.at[chunk],
            send_sem=text_send.at[at],
            recv_sem=text_recv.at[at, min(lane, 1)],
            device_id={"clip": to},
            device_id_type=MESH,
        )

    @pl.when(my_far == 1)
    def _():
        for at in range(2):
            text_copy(at, 0).start()

    for lane in range(1, 4):
        for at in range(2):
            text_copy(at, lane).start()

    def send_one(at):
        def body(slot, carry):
            moved(at, slot).start()
            return carry

        lax.fori_loop(1, PEERS, body, 0)

    send_one(0)
    for at in range(2):
        text_copy(at, 0).wait_recv()

    @pl.when(my_far == 0)
    def _():
        for at in range(2):
            text_copy(at, 0).start()

    for lane in range(4, 7):
        for at in range(2):
            text_copy(at, lane).start()
    send_one(1)

    def send_queries(slot, carry):
        moved(2, slot).start()
        moved(3, slot).start()
        return carry

    lax.fori_loop(1, PEERS, send_queries, 0)

    own_weight.wait()
    weight = w_buf[...]
    for half in range(2):
        for group in range(4):
            channel = lax.broadcasted_iota(jnp.int32, (64, 128), 0) - 32 * half
            lane = lax.broadcasted_iota(jnp.int32, (64, 128), 1) - 32 * group
            chosen = (channel == lane) & (lane >= 0) & (lane < 32)
            chosen = jnp.where(chosen, 1.0, 0.0).astype(jnp.bfloat16)
            spread[pl.ds(group * 128, 128), pl.ds(half * 128, 128)] = lax.dot_general(
                weight, chosen, TN, preferred_element_type=jnp.float32
            ).astype(jnp.bfloat16)

    position = jnp.broadcast_to(step_ref[...], (1, TOKENS)).astype(jnp.float32)
    sigma_now = sigma_at(position)
    sigma_next = sigma_at(position + 1.0)
    lambda_now = log_ratio(sigma_now)
    h_value = log_ratio(sigma_next) - lambda_now
    ratio = (log_ratio(sigma_at(position - 1.0)) - lambda_now) / h_value
    pull = (1.0 - sigma_next) * (jnp.exp(-h_value) - 1.0)
    keep, push = sigma_next / sigma_now, 0.5 * pull / ratio
    text_limit = limit_ref[...]
    coefficient = jnp.where(core == 0, guide_scale, 1.0 - guide_scale)

    for at, buf in enumerate((tk_buf, tv_buf)):
        await_bytes(buf.at[pl.ds(0, 7)], text_recv.at[at, 1])
    for at, buf in enumerate((k_buf, v_buf)):
        await_bytes(buf, whole_recv.at[at])

    def to_partner(pair):
        return pltpu.make_async_remote_copy(
            src_ref=part_out.at[pair],
            dst_ref=part_in.at[pair],
            send_sem=part_send.at[0],
            recv_sem=part_recv.at[pair],
            device_id={"cfg": 1 - core},
            device_id_type=MESH,
        )

    def to_owner(slot):
        return pltpu.make_async_remote_copy(
            src_ref=back_out.at[slot],
            dst_ref=back_in.at[slot],
            send_sem=back_send.at[0],
            recv_sem=back_recv.at[0],
            device_id={"sp": origin(slot)},
            device_id_type=MESH,
        )

    def finish(pair):
        to_partner(pair).wait_recv()
        both = mine[pair] + part_in[pair]
        back_out[2 * pair] = both[:PACK]
        back_out[2 * pair + 1] = both[PACK:]

        @pl.when(pair > 0)
        def _():
            to_owner(2 * pair).start()

        to_owner(2 * pair + 1).start()

    def one_pair(pair, carry):
        for at, buf in enumerate((c_buf, q_buf)):
            await_bytes(buf.at[pl.ds(2 * pair, 2)], pair_recv.at[at, pair])
        rows = 2 * TOKENS
        keys = k_buf[...].reshape(PEERS * TOKENS, HEAD_SIZE)
        values = v_buf[...].reshape(PEERS * TOKENS, HEAD_SIZE)
        queries = q_buf[pl.ds(2 * pair, 2)].reshape(rows, HEAD_SIZE)
        crossing = c_buf[pl.ds(2 * pair, 2)].reshape(rows, HEAD_SIZE)
        prompt_keys = tk_buf[...].reshape(512, HEAD_SIZE)
        prompt_values = tv_buf[...].reshape(512, HEAD_SIZE)
        self_out = attend(queries, keys, values, None)
        cross_out = attend(crossing, prompt_keys, prompt_values, text_limit)
        attended = (self_out + cross_out).astype(jnp.bfloat16).astype(jnp.float32)
        packed = []
        for first in (0, TOKENS):
            groups = [attended[first + PACK * g : first + PACK * (g + 1)] for g in range(3)]
            last = attended[first + 3 * PACK : first + TOKENS]
            padding = jnp.zeros((4 * PACK - TOKENS, HEAD_SIZE), jnp.float32)
            groups.append(jnp.concatenate([last, padding], axis=0))
            packed.append(jnp.concatenate(groups, axis=1))
        packed = jnp.concatenate(packed, axis=0).astype(jnp.bfloat16)
        product = coefficient * jnp.dot(packed, spread[...], preferred_element_type=jnp.float32)
        low, high = product[:, :128], product[:, 128:]
        mine[pair] = jnp.where(core == 0, low, high)
        part_out[pair] = jnp.where(core == 0, high, low)
        to_partner(pair).start()

        @pl.when(pair > 0)
        def _():
            finish(pair - 1)

        return carry

    lax.fori_loop(0, PAIRS, one_pair, 0)
    finish(PAIRS - 1)

    await_bytes(back_in.at[pl.ds(1, PEERS - 1)], back_recv.at[0])
    total = back_out[0] + jnp.sum(back_in[pl.ds(1, PEERS - 1)], axis=0)
    square = jnp.concatenate([total, jnp.zeros((128 - PACK, 128), jnp.float32)], axis=0).T
    token = lax.broadcasted_iota(jnp.int32, (32, 128), 1)
    velocity = square[:32]
    for group in range(1, 4):
        shifted = pltpu.roll(square[32 * group : 32 * (group + 1)], PACK * group, 1)
        velocity = jnp.where(token < PACK * group, velocity, shifted)
    own_latent.wait()
    own_previous.wait()
    latent = latent_buf[...]
    denoised = latent - sigma_now * velocity[:, :TOKENS]
    out_ref[:32] = denoised
    out_ref[32:] = keep * latent - pull * denoised - push * (denoised - previous_buf[...])

    for at, (ref, buf) in enumerate(pairs):
        await_bytes(buf.at[pl.ds(1, PEERS - 1)], send_sem.at[at])
    for at, buf in enumerate((tk_buf, tv_buf)):
        await_bytes(buf.at[pl.ds(0, 7)], text_send.at[at])
    await_bytes(back_out.at[pl.ds(1, PEERS - 1)], back_send.at[0])
    await_bytes(part_out, part_send.at[0])


def on_device(
    self_queries,
    self_keys,
    self_values,
    cross_queries,
    text_keys,
    text_values,
    text_lengths,
    head_weight,
    latent,
    previous_denoised,
    step_index,
):
    flat = lambda array: array.reshape(array.shape[-2], array.shape[-1])
    vmem = pl.BlockSpec(memory_space=pltpu.VMEM)
    anywhere = pl.BlockSpec(memory_space=pl.ANY)
    block = pltpu.VMEM((PEERS, TOKENS, HEAD_SIZE), jnp.bfloat16)
    prompt = pltpu.VMEM((8, 64, HEAD_SIZE), jnp.bfloat16)
    paired = pltpu.VMEM((PAIRS, 2 * PACK, 128), jnp.float32)
    single = pltpu.VMEM((PEERS, PACK, 128), jnp.float32)
    dma = pltpu.SemaphoreType.DMA
    result = pl.pallas_call(
        kernel,
        out_shape=jax.ShapeDtypeStruct((64, TOKENS), jnp.float32),
        in_specs=[vmem] * 2 + [anywhere] * 9,
        out_specs=vmem,
        scratch_shapes=[block] * 4
        + [prompt] * 2
        + [pltpu.VMEM((64, HEAD_SIZE), jnp.bfloat16)]
        + [pltpu.VMEM((32, TOKENS), jnp.float32)] * 2
        + [pltpu.VMEM((512, 256), jnp.bfloat16)]
        + [paired] * 3
        + [single] * 2
        + [dma((4,)), dma((2,)), dma((2, PAIRS)), dma((2,)), dma((2, 2)), dma((3,))]
        + [dma((1,)), dma((PAIRS,)), dma((1,)), dma((1,))],
        compiler_params=pltpu.CompilerParams(
            collective_id=0, has_side_effects=True, vmem_limit_bytes=62 * 2**20
        ),
        name="denoise",
    )(
        text_lengths.reshape(1, 1),
        step_index.reshape(1, 1),
        flat(self_queries),
        flat(self_keys),
        flat(self_values),
        flat(cross_queries),
        flat(text_keys),
        flat(text_values),
        head_weight.T,
        flat(latent).T,
        flat(previous_denoised).T,
    )
    return (result[:32].T[None], result[32:].T[None])


def solution(mesh):
    return jax.shard_map(
        on_device,
        mesh=mesh,
        in_specs=(
            P("clip", "cfg", "sp", None),
            P("clip", "cfg", "sp", None),
            P("clip", "cfg", "sp", None),
            P("clip", "cfg", "sp", None),
            P("cfg", "clip", "sp"),
            P("cfg", "clip", "sp"),
            P("cfg"),
            P(),
            P("clip", "sp", "cfg"),
            P("clip", "sp", "cfg"),
            P("clip"),
        ),
        out_specs=(P("clip", "sp", "cfg"), P("clip", "sp", "cfg")),
        check_vma=False,
    )
```
